32 devices in a mesh: dp: 8 (over y, x, core), seq: 4 (over z).
Axes of the slice: x: 2, y: 2, z: 4, core: 2. Of those that a mesh axis runs over, the one named last changes fastest.
Arguments:
- enc_hidden: bfloat16 [8, 256, 5120], P('dp', None, 'seq'), may hold values from -6 to 6
- enc_wo: bfloat16 [5120, 4096], P('seq'), may hold values from -0.078125 to 0.078125
- enc_gain: float32 [4096], replicated, may hold values from 0.25 to 1.75
- text_len: int32 [8], P('dp'), may hold values from 1 to 256, as said below
- text_kv: bfloat16 [4096, 2, 2048], P(None, None, 'seq'), may hold values from -0.09375 to 0.09375
- lat_qkv: bfloat16 [8, 1024, 3, 2048], P('dp', 'seq')
- output_weight: bfloat16 [2048, 3072], P('seq'), may hold values from -0.125 to 0.125
- output_cotangent: bfloat16 [8, 1024, 3072], P('dp', 'seq'), may hold values from -6 to 6
Outputs:
- latent_block_output: bfloat16 [8, 1024, 3072], P('dp', 'seq')
- output_weight_gradient: float32 [2048, 3072], P('seq', 'dp')
The draws below stay inside these ranges and needn't reach their ends.
Inputs may be any that keep to these rules, and one draw needn't show every extreme that they name: `text_len`: some sample has all 256 text tokens.
All inputs are finite; a program needn't handle non-finite values.
Results may differ from the reference program's by a relative error of at most 0.018.
Values may be sent and summed in bfloat16 or wider, within the bound.
A program may use at most 128 MiB of HBM per device.

```python
import jax
import jax.numpy as jnp
from jax import lax

D = 3072
HEADS = 16
HD = 128
ENC = 4096
EFF = 5120
TXT = 256
HW = 2048
LAT = 1024
NS = 8
N_SEQ = 4


def draw_text_len(key, part):
    key = jax.random.fold_in(key, 7)
    counts = jax.random.randint(key, (NS,), 1, TXT + 1)
    longest = jax.random.randint(jax.random.fold_in(key, 1), (), 0, NS)
    return jnp.where(jnp.arange(NS) == longest, TXT, counts).astype(jnp.int32)


def draw_lat_qkv(key, part):
    key = jax.random.fold_in(key, 11)
    base = jax.random.normal(key, (NS, LAT, 3, HW), jnp.float32)
    return base.astype(jnp.bfloat16)


def shard_levels(own_key, extent, shards, low, top_value):
    def one(position, shards_of):
        steps = jax.random.uniform(jax.random.fold_in(jax.random.fold_in(own_key, 6), position), (shards_of,), jnp.float32, low / len(shards), top_value / len(shards))
        return jnp.repeat(jnp.exp(steps), extent[position] // shards_of).reshape((-1,) + (1,) * (len(extent) - position - 1))

    loudness = one(*shards[0])
    for cut in shards[1:]:
        loudness = loudness * one(*cut)
    return loudness


def scatter_about(stream_key, extent, scale, bound, pieces=(), kind=jnp.bfloat16):
    values = scale * jax.random.normal(stream_key, extent, jnp.float32)
    if pieces:
        values = values * shard_levels(stream_key, extent, pieces, -0.22, 0.18)
    return jnp.clip(values, -bound, bound).astype(kind)


def setup_inputs(seed: int = 0) -> dict:
    arg_keys = jax.random.split(jax.random.key(seed), 9)
    return {
        "enc_hidden": scatter_about(arg_keys[0], (NS, TXT, EFF), 1.0, 6.0, ((0, 8), (2, 4))),
        "enc_wo": scatter_about(arg_keys[1], (EFF, ENC), EFF ** -0.5, 0.078125, ((0, 4),)),
        "enc_gain": jnp.clip(1.0 + 0.15 * jax.random.normal(arg_keys[2], (ENC,), jnp.float32), 0.25, 1.75),
        "text_len": draw_text_len(jax.random.fold_in(arg_keys[8], 71), 0),
        "text_kv": scatter_about(arg_keys[4], (ENC, 2, HW), ENC ** -0.5, 0.09375, ((2, 4),)),
        "lat_qkv": draw_lat_qkv(jax.random.fold_in(arg_keys[8], 71), 0),
        "output_weight": scatter_about(arg_keys[6], (HW, D), HW ** -0.5, 0.125, ((0, 4),)),
        "output_cotangent": scatter_about(arg_keys[7], (NS, LAT, D), 1.0, 6.0, ((0, 8), (1, 4))),
    }


def one_sample(items):
    qkv, text_pair, sequence_length = items
    queries = qkv[:, 0].astype(jnp.float32).reshape(LAT, HEADS, HD)
    keys = jnp.concatenate([qkv[:, 1], text_pair[:, 0]], 0).astype(jnp.float32).reshape(LAT + TXT, HEADS, HD)
    values = jnp.concatenate([qkv[:, 2], text_pair[:, 1]], 0).astype(jnp.float32).reshape(LAT + TXT, HEADS, HD)
    keep = jnp.concatenate([jnp.ones((LAT,), bool), jnp.arange(TXT) < sequence_length])
    scores = jnp.einsum('qhd,khd->hqk', queries, keys) * HD ** (-0.5)
    scores = jnp.where(keep[None, None, :], scores, -1e+30)
    top = lax.optimization_barrier(jnp.max(scores, -1, keepdims=True))
    weights = jnp.exp(scores - top)
    probs = (weights / lax.optimization_barrier(jnp.sum(weights, -1, keepdims=True))).astype(jnp.bfloat16)
    probs = lax.optimization_barrier(probs).astype(jnp.float32)
    attn = jnp.einsum('hqk,khd->qhd', probs, values)
    return attn.reshape(LAT, HW).astype(jnp.bfloat16)

def reference(enc_hidden, enc_wo, enc_gain, text_len, text_kv, lat_qkv, output_weight, output_cotangent):
    width = EFF // N_SEQ
    enc_out = jnp.zeros((NS, TXT, ENC), jnp.float32)
    for shard in range(N_SEQ):
        block = enc_hidden[:, :, shard * width:(shard + 1) * width].astype(jnp.float32)
        weight = enc_wo[shard * width:(shard + 1) * width].astype(jnp.float32)
        partial_value = jnp.einsum('ste,ed->std', block, weight).astype(jnp.bfloat16)
        enc_out = enc_out + lax.optimization_barrier(partial_value).astype(jnp.float32)
    meansq = lax.optimization_barrier(jnp.mean(enc_out * enc_out, -1, keepdims=True))
    text_emb = (enc_out * lax.rsqrt(meansq + 1e-06) * enc_gain).astype(jnp.bfloat16)
    text_pairs = jnp.einsum('std,dkh->stkh', text_emb.astype(jnp.float32), text_kv.astype(jnp.float32)).astype(jnp.bfloat16)
    attn = lax.map(one_sample, (lat_qkv, text_pairs, text_len))
    attention_width_full = attn.astype(jnp.float32)
    latent_block_output = jnp.einsum('ugj,jn->ugn', attention_width_full, output_weight.astype(jnp.float32)).astype(jnp.bfloat16)
    output_weight_gradient = jnp.einsum('vwk,vwy->ky', attention_width_full, output_cotangent.astype(jnp.float32))
    return (latent_block_output, output_weight_gradient)
```

```python
import jax
import jax.numpy as jnp
from jax import lax
from jax.sharding import PartitionSpec as P

HD = 128


def encoder_text(enc_hidden, enc_wo, enc_gain):
    partial_value = jnp.einsum(
        "ste,ed->std", enc_hidden, enc_wo, preferred_element_type=jnp.float32
    ).astype(jnp.bfloat16)
    summed = lax.psum(partial_value, "seq").astype(jnp.float32)
    meansq = jnp.mean(summed * summed, -1, keepdims=True)
    return (summed * lax.rsqrt(meansq + 1e-06) * enc_gain).astype(jnp.bfloat16)


def attend(gathered, text_pairs, text_len):
    samples, latent, _, local_width = gathered.shape
    heads_here = local_width // HD
    text_count = text_pairs.shape[1]
    keys = jnp.concatenate([gathered[:, :, 1], text_pairs[:, :, 0]], 1)
    keys = keys.reshape(samples, latent + text_count, heads_here, HD)
    values = jnp.concatenate([gathered[:, :, 2], text_pairs[:, :, 1]], 1)
    values = values.reshape(samples, latent + text_count, heads_here, HD)
    keep = jnp.concatenate(
        [jnp.ones((samples, latent), bool), jnp.arange(text_count)[None, :] < text_len[:, None]], 1
    )
    block_rows = min(512, latent)
    queries = gathered[:, :, 0].reshape(samples, latent // block_rows, block_rows, heads_here, HD)
    queries = jnp.moveaxis(queries, 1, 0)

    def one_block(query_block):
        scores = jnp.einsum(
            "sqhd,skhd->shqk", query_block, keys, preferred_element_type=jnp.float32
        ) * HD ** (-0.5)
        scores = jnp.where(keep[:, None, None, :], scores, -1e30)
        top = jnp.max(scores, -1, keepdims=True)
        weights = jnp.exp(scores - top)
        probs = (weights / jnp.sum(weights, -1, keepdims=True)).astype(jnp.bfloat16)
        result = jnp.einsum("shqk,skhd->sqhd", probs, values, preferred_element_type=jnp.float32)
        return result.reshape(samples, block_rows, local_width).astype(jnp.bfloat16)

    block_count = lax.map(one_block, queries)
    return jnp.moveaxis(block_count, 0, 1).reshape(samples, latent, local_width)


def shards(
    enc_hidden, enc_wo, enc_gain, text_len, text_kv, lat_qkv, output_weight, output_cotangent
):
    text_emb = encoder_text(enc_hidden, enc_wo, enc_gain)
    share = output_weight.shape[0] // lax.axis_size("dp")
    rows = lax.dynamic_slice_in_dim(output_weight, lax.axis_index("dp") * share, share, 0)
    rows, text_emb = lax.optimization_barrier((rows, text_emb))
    weight = lax.all_gather(rows, ("seq", "dp"), axis=0, tiled=True)
    text_pairs = jnp.einsum(
        "std,dkh->stkh", text_emb, text_kv, preferred_element_type=jnp.float32
    ).astype(jnp.bfloat16)
    gathered = lax.all_to_all(lat_qkv, "seq", split_axis=3, concat_axis=1, tiled=True)
    attn_heads = attend(gathered, text_pairs, text_len)
    attention_token_rows = lax.all_to_all(
        attn_heads, "seq", split_axis=1, concat_axis=2, tiled=True
    )
    attention_token_rows, weight = lax.optimization_barrier((attention_token_rows, weight))
    columns = attention_token_rows
    projected = jnp.einsum(
        "ugj,jn->ugn",
        columns,
        weight,
        preferred_element_type=jnp.float32,
    )
    latent_block_output = projected.astype(jnp.bfloat16)
    partial_value = jnp.einsum(
        "vwk,vwy->yk", attention_token_rows, output_cotangent, preferred_element_type=jnp.float32
    )
    columns = lax.psum_scatter(
        partial_value.astype(jnp.bfloat16), "dp", scatter_dimension=0, tiled=True
    )
    output_weight_gradient = lax.psum_scatter(
        columns.T, "seq", scatter_dimension=0, tiled=True
    ).astype(jnp.float32)
    return (latent_block_output, output_weight_gradient)


def solution(mesh):
    placed = (
        P("dp", None, "seq"),
        P("seq", None),
        P(),
        P("dp"),
        P(None, None, "seq"),
        P("dp", "seq", None, None),
        P("seq", None),
        P("dp", "seq", None),
    )
    return jax.shard_map(
        shards,
        mesh=mesh,
        in_specs=placed,
        out_specs=(P("dp", "seq", None), P("seq", "dp")),
        check_vma=False,
    )
```

```python
import functools
import math

import jax
import jax.numpy as jnp
from jax import lax
from jax.experimental import pallas as pl
from jax.experimental.pallas import tpu as pltpu
from jax.sharding import PartitionSpec as P

HD = 128
MESH = pl.DeviceIdType.MESH
ANY = pl.BlockSpec(memory_space=pl.ANY)


def collect_kernel(n, chips, qkv, rows, heads, weight, z_s, z_r, q_s, q_r, p_s, p_r, c_s, c_r, own):
    me, dp = lax.axis_index("seq"), lax.axis_index("dp")
    chip, core = dp // 2, dp % 2
    other = 2 * chip + 1 - core
    tokens = qkv.shape[1]
    width = heads.shape[2]
    block = rows.shape[0]
    share = block // (2 * chips)

    barrier = pltpu.get_barrier_semaphore()
    for k in range(1, n):
        to = lax.rem(me + k, n)
        pl.semaphore_signal(barrier, inc=1, device_id=(dp, to), device_id_type=MESH)
    for k in range(1, chips):
        to = 2 * lax.rem(chip + k, chips) + core
        pl.semaphore_signal(barrier, inc=1, device_id=(to, me), device_id_type=MESH)
    pl.semaphore_signal(barrier, inc=1, device_id=(other, me), device_id_type=MESH)
    pl.semaphore_wait(barrier, n - 1 + chips - 1 + 1)

    def remote(src, dst, send, recv, to):
        return pltpu.make_async_remote_copy(
            src_ref=src, dst_ref=dst, send_sem=send, recv_sem=recv, device_id=to, device_id_type=MESH
        )

    def piece(s, d):
        start = pl.multiple_of(s * block + d * share, share)
        return weight.at[pl.ds(start, share)]

    def columns(s):
        return pl.ds(pl.multiple_of(s * width, width), width)

    mine = pl.ds(pl.multiple_of(me * tokens, tokens), tokens)
    fetch, tokens_out = [], []
    for k in range(1, n):
        to = lax.rem(me + k, n)
        fetch.append(
            remote(
                rows.at[pl.ds(pl.multiple_of(dp * share, share), share)],
                piece(me, dp), z_s.at[k - 1], z_r.at[k - 1], (dp, to),
            )
        )
        fetch[-1].start()
    for k in range(1, n):
        to = lax.rem(me + k, n)
        tokens_out.append(
            remote(
                qkv.at[:, :, columns(to)], heads.at[:, mine], q_s.at[k - 1], q_r.at[k - 1], (dp, to)
            )
        )
        tokens_out[-1].start()
    stay = [
        pltpu.make_async_copy(qkv.at[:, :, columns(me)], heads.at[:, mine], own.at[0]),
        pltpu.make_async_copy(
            rows, weight.at[pl.ds(pl.multiple_of(me * block, block), block)], own.at[1]
        ),
    ]
    for copy in stay:
        copy.start()

    plane, cores = [], []
    for k in range(1, n):
        fetch[k - 1].wait_recv()
        source = lax.rem(me - k + n, n)
        held = piece(source, dp)
        for c in range(1, chips):
            to = 2 * lax.rem(chip + c, chips) + core
            plane.append(remote(held, held, p_s.at[k - 1, c - 1], p_r.at[k - 1, c - 1], (to, me)))
            plane[-1].start()
        cores.append(remote(held, held, c_s.at[k - 1, 0], c_r.at[k - 1, 0], (other, me)))
        cores[-1].start()
    for k in range(1, n):
        source = lax.rem(me - k + n, n)
        for c in range(1, chips):
            plane[(k - 1) * (chips - 1) + c - 1].wait_recv()
            held = piece(source, 2 * lax.rem(chip - c + chips, chips) + core)
            cores.append(remote(held, held, c_s.at[k - 1, c], c_r.at[k - 1, c], (other, me)))
            cores[-1].start()
    for copy in fetch + plane:
        copy.wait_send()
    for copy in cores + tokens_out + stay:
        copy.wait()


def collect(lat_qkv, output_weight):
    n, chips = lax.axis_size("seq"), lax.axis_size("dp") // 2
    _, tokens, _, wide = lat_qkv.shape
    block, features = output_weight.shape
    dma = pltpu.SemaphoreType.DMA
    return pl.pallas_call(
        functools.partial(collect_kernel, n, chips),
        out_shape=(
            jax.ShapeDtypeStruct((3, n * tokens, wide // n), lat_qkv.dtype),
            jax.ShapeDtypeStruct((n * block, features), output_weight.dtype),
        ),
        in_specs=[ANY, ANY],
        out_specs=(ANY, ANY),
        scratch_shapes=[
            dma((n - 1,)), dma((n - 1,)), dma((n - 1,)), dma((n - 1,)),
            dma((n - 1, chips - 1)), dma((n - 1, chips - 1)),
            dma((n - 1, chips)), dma((n - 1, chips)), dma((2,)),
        ],
        compiler_params=pltpu.CompilerParams(collective_id=0, has_side_effects=True),
        cost_estimate=pl.CostEstimate(flops=0, bytes_accessed=300_000_000, transcendentals=0),
    )(jnp.transpose(lat_qkv[0], (1, 0, 2)), output_weight)


def return_kernel(n, attn, rows, send, recv, own):
    me, dp = lax.axis_index("seq"), lax.axis_index("dp")
    tokens, width = rows.shape[0], attn.shape[1]
    barrier = pltpu.get_barrier_semaphore()
    for k in range(1, n):
        to = lax.rem(me + k, n)
        pl.semaphore_signal(barrier, inc=1, device_id=(dp, to), device_id_type=MESH)
    pl.semaphore_wait(barrier, n - 1)
    mine = rows.at[:, pl.ds(pl.multiple_of(me * width, width), width)]

    def part(s):
        return attn.at[pl.ds(pl.multiple_of(s * tokens, tokens), tokens)]

    copies = []
    for k in range(1, n):
        to = lax.rem(me + k, n)
        copies.append(
            pltpu.make_async_remote_copy(
                src_ref=part(to), dst_ref=mine, send_sem=send.at[k - 1], recv_sem=recv.at[k - 1],
                device_id=(dp, to), device_id_type=MESH,
            )
        )
    copies.append(pltpu.make_async_copy(part(me), mine, own))
    for copy in copies:
        copy.start()
    for copy in copies:
        copy.wait()


def give_back(attn):
    n = lax.axis_size("seq")
    latent, width = attn.shape
    dma = pltpu.SemaphoreType.DMA
    return pl.pallas_call(
        functools.partial(return_kernel, n),
        out_shape=jax.ShapeDtypeStruct((latent // n, width * n), attn.dtype),
        in_specs=[ANY],
        out_specs=ANY,
        scratch_shapes=[dma((n - 1,)), dma((n - 1,)), dma],
        compiler_params=pltpu.CompilerParams(collective_id=1, has_side_effects=True),
        cost_estimate=pl.CostEstimate(flops=0, bytes_accessed=60_000_000, transcendentals=0),
    )(attn)


def attend_kernel(length, q, k, v, text_k, text_v, out):
    turned = (((1,), (1,)), ((), ()))
    query = q[0]
    latent = lax.dot_general(query, k[0], turned, preferred_element_type=jnp.float32)
    text = lax.dot_general(query, text_k[0], turned, preferred_element_type=jnp.float32)
    place = lax.broadcasted_iota(jnp.int32, text.shape, 1)
    text = jnp.where(place < length[0], text, -1e30)
    top = jnp.maximum(jnp.max(latent, -1, keepdims=True), jnp.max(text, -1, keepdims=True))
    scale = HD ** (-0.5) * math.log2(math.e)
    latent = jnp.exp2((latent - top) * scale)
    text = jnp.exp2((text - top) * scale)
    total = jnp.sum(latent, -1, keepdims=True) + jnp.sum(text, -1, keepdims=True)
    result = jnp.dot(latent.astype(jnp.bfloat16), v[0], preferred_element_type=jnp.float32)
    result += jnp.dot(text.astype(jnp.bfloat16), text_v[0], preferred_element_type=jnp.float32)
    out[...] = (result / total).astype(out.dtype)


def attend(heads, text, text_len):
    _, latent, width = heads.shape
    count = text.shape[1]
    rows = min(512, latent)

    def block(index, size):
        return pl.BlockSpec((1, size, HD), lambda h, i: (index, 0, h))

    return pl.pallas_call(
        attend_kernel,
        grid=(width // HD, latent // rows),
        in_specs=[
            pl.BlockSpec(memory_space=pltpu.SMEM),
            pl.BlockSpec((1, rows, HD), lambda h, i: (0, i, h)),
            block(1, latent), block(2, latent), block(0, count), block(1, count),
        ],
        out_specs=pl.BlockSpec((rows, HD), lambda h, i: (i, h)),
        out_shape=jax.ShapeDtypeStruct((latent, width), jnp.bfloat16),
        compiler_params=pltpu.CompilerParams(vmem_limit_bytes=40 * 2**20),
    )(text_len, heads, heads, heads, text, text)


def gradient_kernel(attn, cotangent, out):
    product = lax.dot_general(
        attn[...], cotangent[...], (((0,), (0,)), ((), ())), preferred_element_type=jnp.float32
    ).astype(out.dtype)
    width = out.shape[2]
    for part in range(out.shape[0]):
        out[part] = product[:, part * width : (part + 1) * width]


def gradient(attn, cotangent, parts):
    tokens, wide = attn.shape
    features = cotangent.shape[1]
    width = features // parts
    rows = min(256, wide)
    return pl.pallas_call(
        gradient_kernel,
        grid=(wide // rows,),
        in_specs=[
            pl.BlockSpec((tokens, rows), lambda r: (0, r)),
            pl.BlockSpec((tokens, features), lambda r: (0, 0)),
        ],
        out_specs=pl.BlockSpec((parts, rows, width), lambda r: (0, r, 0)),
        out_shape=jax.ShapeDtypeStruct((parts, wide, width), jnp.bfloat16),
        compiler_params=pltpu.CompilerParams(vmem_limit_bytes=40 * 2**20),
    )(attn, cotangent)


def shards(
    enc_hidden, enc_wo, enc_gain, text_len, text_kv, lat_qkv, output_weight, output_cotangent
):
    partial_value = jnp.dot(
        enc_hidden[0], enc_wo, preferred_element_type=jnp.float32
    ).astype(jnp.bfloat16)
    partial_value, lat_qkv = lax.optimization_barrier((partial_value, lat_qkv))
    summed = lax.psum(partial_value, "seq")
    heads, weight = collect(lat_qkv, output_weight)
    summed = summed.astype(jnp.float32)
    meansq = jnp.mean(summed * summed, -1, keepdims=True)
    text_emb = (summed * lax.rsqrt(meansq + 1e-06) * enc_gain).astype(jnp.bfloat16)
    text = jnp.einsum(
        "td,dkh->kth", text_emb, text_kv, preferred_element_type=jnp.float32
    ).astype(jnp.bfloat16)
    rows = give_back(attend(heads, text, text_len))
    parts = gradient(rows, output_cotangent[0], lax.axis_size("dp"))
    columns = lax.psum_scatter(parts, "dp", scatter_dimension=0, tiled=False)
    output_weight_gradient = lax.psum_scatter(
        columns, "seq", scatter_dimension=0, tiled=True
    ).astype(jnp.float32)
    projected = jnp.dot(rows, weight, preferred_element_type=jnp.float32)
    return (projected.astype(jnp.bfloat16)[None], output_weight_gradient)


def solution(mesh):
    placed = (
        P("dp", None, "seq"),
        P("seq", None),
        P(),
        P("dp"),
        P(None, None, "seq"),
        P("dp", "seq", None, None),
        P("seq", None),
        P("dp", "seq", None),
    )
    return jax.shard_map(
        shards,
        mesh=mesh,
        in_specs=placed,
        out_specs=(P("dp", "seq", None), P("seq", "dp")),
        check_vma=False,
    )
```

```python
import functools
import math

import jax
import jax.numpy as jnp
from jax import lax
from jax.experimental import pallas as pl
from jax.experimental.pallas import tpu as pltpu
from jax.sharding import PartitionSpec as P

HD = 128
MESH = pl.DeviceIdType.MESH
ANY = pl.BlockSpec(memory_space=pl.ANY)


def collect_kernel(n, chips, qkv, rows, heads, weight, z_s, z_r, q_s, q_r, p_s, p_r, c_s, c_r, own):
    me, dp = lax.axis_index("seq"), lax.axis_index("dp")
    chip, core = dp // 2, dp % 2
    other = 2 * chip + 1 - core
    tokens = qkv.shape[1]
    width = heads.shape[2]
    block = rows.shape[0]
    share = block // (2 * chips)

    barrier = pltpu.get_barrier_semaphore()
    for k in range(1, n):
        to = lax.rem(me + k, n)
        pl.semaphore_signal(barrier, inc=1, device_id=(dp, to), device_id_type=MESH)
    for k in range(1, chips):
        to = 2 * lax.rem(chip + k, chips) + core
        pl.semaphore_signal(barrier, inc=1, device_id=(to, me), device_id_type=MESH)
    pl.semaphore_signal(barrier, inc=1, device_id=(other, me), device_id_type=MESH)
    pl.semaphore_wait(barrier, n - 1 + chips - 1 + 1)

    def remote(src, dst, send, recv, to):
        return pltpu.make_async_remote_copy(
            src_ref=src, dst_ref=dst, send_sem=send, recv_sem=recv, device_id=to, device_id_type=MESH
        )

    def piece(s, d):
        start = pl.multiple_of(s * block + d * share, share)
        return weight.at[pl.ds(start, share)]

    def columns(s):
        return pl.ds(pl.multiple_of(s * width, width), width)

    mine = pl.ds(pl.multiple_of(me * tokens, tokens), tokens)
    fetch, tokens_out = [], []
    for k in range(1, n):
        to = lax.rem(me + k, n)
        fetch.append(
            remote(
                rows.at[pl.ds(pl.multiple_of(dp * share, share), share)],
                piece(me, dp), z_s.at[k - 1], z_r.at[k - 1], (dp, to),
            )
        )
        fetch[-1].start()
    for k in range(1, n):
        to = lax.rem(me + k, n)
        tokens_out.append(
            remote(
                qkv.at[:, :, columns(to)], heads.at[:, mine], q_s.at[k - 1], q_r.at[k - 1], (dp, to)
            )
        )
        tokens_out[-1].start()
    stay = [
        pltpu.make_async_copy(qkv.at[:, :, columns(me)], heads.at[:, mine], own.at[0]),
        pltpu.make_async_copy(
            rows, weight.at[pl.ds(pl.multiple_of(me * block, block), block)], own.at[1]
        ),
    ]
    for copy in stay:
        copy.start()

    plane, cores = [], []
    for k in range(1, n):
        fetch[k - 1].wait_recv()
        source = lax.rem(me - k + n, n)
        held = piece(source, dp)
        for c in range(1, chips):
            to = 2 * lax.rem(chip + c, chips) + core
            plane.append(remote(held, held, p_s.at[k - 1, c - 1], p_r.at[k - 1, c - 1], (to, me)))
            plane[-1].start()
        cores.append(remote(held, held, c_s.at[k - 1, 0], c_r.at[k - 1, 0], (other, me)))
        cores[-1].start()
    for k in range(1, n):
        source = lax.rem(me - k + n, n)
        for c in range(1, chips):
            plane[(k - 1) * (chips - 1) + c - 1].wait_recv()
            held = piece(source, 2 * lax.rem(chip - c + chips, chips) + core)
            cores.append(remote(held, held, c_s.at[k - 1, c], c_r.at[k - 1, c], (other, me)))
            cores[-1].start()
    for copy in fetch + plane:
        copy.wait_send()
    for copy in cores + tokens_out + stay:
        copy.wait()


def collect(lat_qkv, output_weight):
    n, chips = lax.axis_size("seq"), lax.axis_size("dp") // 2
    _, tokens, _, wide = lat_qkv.shape
    block, features = output_weight.shape
    dma = pltpu.SemaphoreType.DMA
    return pl.pallas_call(
        functools.partial(collect_kernel, n, chips),
        out_shape=(
            jax.ShapeDtypeStruct((3, n * tokens, wide // n), lat_qkv.dtype),
            jax.ShapeDtypeStruct((n * block, features), output_weight.dtype),
        ),
        in_specs=[ANY, ANY],
        out_specs=(ANY, ANY),
        scratch_shapes=[
            dma((n - 1,)), dma((n - 1,)), dma((n - 1,)), dma((n - 1,)),
            dma((n - 1, chips - 1)), dma((n - 1, chips - 1)),
            dma((n - 1, chips)), dma((n - 1, chips)), dma((2,)),
        ],
        compiler_params=pltpu.CompilerParams(collective_id=0, has_side_effects=True),
        cost_estimate=pl.CostEstimate(flops=0, bytes_accessed=300_000_000, transcendentals=0),
    )(jnp.transpose(lat_qkv[0], (1, 0, 2)), output_weight)


def return_kernel(n, attn, rows, send, recv, own):
    me, dp = lax.axis_index("seq"), lax.axis_index("dp")
    tokens, width = rows.shape[0], attn.shape[1]
    barrier = pltpu.get_barrier_semaphore()
    for k in range(1, n):
        to = lax.rem(me + k, n)
        pl.semaphore_signal(barrier, inc=1, device_id=(dp, to), device_id_type=MESH)
    pl.semaphore_wait(barrier, n - 1)
    mine = rows.at[:, pl.ds(pl.multiple_of(me * width, width), width)]

    def part(s):
        return attn.at[pl.ds(pl.multiple_of(s * tokens, tokens), tokens)]

    copies = []
    for k in range(1, n):
        to = lax.rem(me + k, n)
        copies.append(
            pltpu.make_async_remote_copy(
                src_ref=part(to), dst_ref=mine, send_sem=send.at[k - 1], recv_sem=recv.at[k - 1],
                device_id=(dp, to), device_id_type=MESH,
            )
        )
    copies.append(pltpu.make_async_copy(part(me), mine, own))
    for copy in copies:
        copy.start()
    for copy in copies:
        copy.wait()


def give_back(attn):
    n = lax.axis_size("seq")
    latent, width = attn.shape
    dma = pltpu.SemaphoreType.DMA
    return pl.pallas_call(
        functools.partial(return_kernel, n),
        out_shape=jax.ShapeDtypeStruct((latent // n, width * n), attn.dtype),
        in_specs=[ANY],
        out_specs=ANY,
        scratch_shapes=[dma((n - 1,)), dma((n - 1,)), dma],
        compiler_params=pltpu.CompilerParams(collective_id=1, has_side_effects=True),
        cost_estimate=pl.CostEstimate(flops=0, bytes_accessed=60_000_000, transcendentals=0),
    )(attn)


def attend_kernel(length, q, k, v, text_k, text_v, out):
    turned = (((1,), (1,)), ((), ()))
    query = q[0]
    latent = lax.dot_general(query, k[0], turned, preferred_element_type=jnp.float32)
    text = lax.dot_general(query, text_k[0], turned, preferred_element_type=jnp.float32)
    place = lax.broadcasted_iota(jnp.int32, text.shape, 1)
    text = jnp.where(place < length[0], text, -1e30)
    top = jnp.maximum(jnp.max(latent, -1, keepdims=True), jnp.max(text, -1, keepdims=True))
    scale = HD ** (-0.5) * math.log2(math.e)
    latent = jnp.exp2((latent - top) * scale)
    text = jnp.exp2((text - top) * scale)
    total = jnp.sum(latent, -1, keepdims=True) + jnp.sum(text, -1, keepdims=True)
    result = jnp.dot(latent.astype(jnp.bfloat16), v[0], preferred_element_type=jnp.float32)
    result += jnp.dot(text.astype(jnp.bfloat16), text_v[0], preferred_element_type=jnp.float32)
    out[...] = (result / total).astype(out.dtype)


def attend(heads, text, text_len):
    _, latent, width = heads.shape
    count = text.shape[1]
    rows = min(512, latent)

    def block(index, size):
        return pl.BlockSpec((1, size, HD), lambda h, i: (index, 0, h))

    return pl.pallas_call(
        attend_kernel,
        grid=(width // HD, latent // rows),
        in_specs=[
            pl.BlockSpec(memory_space=pltpu.SMEM),
            pl.BlockSpec((1, rows, HD), lambda h, i: (0, i, h)),
            block(1, latent), block(2, latent), block(0, count), block(1, count),
        ],
        out_specs=pl.BlockSpec((rows, HD), lambda h, i: (i, h)),
        out_shape=jax.ShapeDtypeStruct((latent, width), jnp.bfloat16),
        compiler_params=pltpu.CompilerParams(vmem_limit_bytes=40 * 2**20),
    )(text_len, heads, heads, heads, text, text)


def gradient_kernel(
    chips, attn, cotangent, out, turned, give, got, keep, land, g_s, g_r, k_s, k_r
):
    me, dp = lax.axis_index("seq"), lax.axis_index("dp")
    chip, core = dp // 2, dp % 2
    other = 2 * chip + 1 - core
    wide = out.shape[0]
    tile = math.gcd(wide, 512)

    barrier = pltpu.get_barrier_semaphore()
    for k in range(1, chips):
        to = 2 * lax.rem(chip + k, chips) + core
        pl.semaphore_signal(barrier, inc=1, device_id=(to, me), device_id_type=MESH)
    pl.semaphore_signal(barrier, inc=1, device_id=(other, me), device_id_type=MESH)
    turned[...] = attn[...].T
    pl.semaphore_wait(barrier, chips)

    def remote(src, dst, send, recv, to):
        return pltpu.make_async_remote_copy(
            src_ref=src, dst_ref=dst, send_sem=send, recv_sem=recv, device_id=to, device_id_type=MESH
        )

    def tiles(body):
        def step(t, carry):
            body(pl.ds(pl.multiple_of(t * tile, tile), tile))
            return carry

        lax.fori_loop(0, wide // tile, step, 0)

    def term(rows, index):
        return jnp.dot(turned[rows, :], cotangent[index], preferred_element_type=jnp.float32)

    order = list(range(1, chips)) + [0]
    gives, keeps = {}, []
    for k in order:
        index = 2 * lax.rem(chip + k, chips) + 1 - core

        def fill(rows):
            give[k, rows, :] = term(rows, index).astype(give.dtype)

        tiles(fill)
        gives[k] = remote(give.at[k], got.at[k], g_s.at[k], g_r.at[k], (other, me))
        gives[k].start()
    for k in range(1, chips):
        index = 2 * lax.rem(chip + k, chips) + core
        gives[k].wait_recv()

        def add(rows):
            both = term(rows, index) + got[k, rows, :].astype(jnp.float32)
            keep[k - 1, rows, :] = both.astype(keep.dtype)

        tiles(add)
        keeps.append(remote(keep.at[k - 1], land.at[k - 1], k_s.at[k - 1], k_r.at[k - 1], (index, me)))
        keeps[-1].start()
    gives[0].wait_recv()
    for copy in keeps:
        copy.wait_recv()

    def finish(rows):
        total = term(rows, dp) + got[0, rows, :].astype(jnp.float32)
        for k in range(1, chips):
            total += land[k - 1, rows, :].astype(jnp.float32)
        out[rows, :] = total.astype(out.dtype)

    tiles(finish)
    for copy in list(gives.values()) + keeps:
        copy.wait_send()


def gradient(attn, cotangent):
    parts = lax.axis_size("dp")
    chips = parts // 2
    tokens, wide = attn.shape
    width = cotangent.shape[1] // parts
    cotangent = jnp.transpose(cotangent.reshape(tokens, parts, width), (1, 0, 2))
    vmem = pl.BlockSpec(memory_space=pltpu.VMEM)
    dma = pltpu.SemaphoreType.DMA
    return pl.pallas_call(
        functools.partial(gradient_kernel, chips),
        in_specs=[vmem, vmem],
        out_specs=vmem,
        out_shape=jax.ShapeDtypeStruct((wide, width), jnp.bfloat16),
        scratch_shapes=[
            pltpu.VMEM((wide, tokens), jnp.bfloat16),
            pltpu.VMEM((chips, wide, width), jnp.bfloat16),
            pltpu.VMEM((chips, wide, width), jnp.bfloat16),
            pltpu.VMEM((chips - 1, wide, width), jnp.bfloat16),
            pltpu.VMEM((chips - 1, wide, width), jnp.bfloat16),
            dma((chips,)), dma((chips,)), dma((chips - 1,)), dma((chips - 1,)),
        ],
        compiler_params=pltpu.CompilerParams(
            collective_id=2, has_side_effects=True, vmem_limit_bytes=52 * 2**20
        ),
        cost_estimate=pl.CostEstimate(flops=0, bytes_accessed=200_000_000, transcendentals=0),
    )(attn, cotangent)


def shards(
    enc_hidden, enc_wo, enc_gain, text_len, text_kv, lat_qkv, output_weight, output_cotangent
):
    partial_value = jnp.dot(
        enc_hidden[0], enc_wo, preferred_element_type=jnp.float32
    ).astype(jnp.bfloat16)
    partial_value, lat_qkv = lax.optimization_barrier((partial_value, lat_qkv))
    summed = lax.psum(partial_value, "seq")
    heads, weight = collect(lat_qkv, output_weight)
    heads, output_cotangent = lax.optimization_barrier((heads, output_cotangent))
    summed = summed.astype(jnp.float32)
    meansq = jnp.mean(summed * summed, -1, keepdims=True)
    text_emb = (summed * lax.rsqrt(meansq + 1e-06) * enc_gain).astype(jnp.bfloat16)
    text = jnp.einsum(
        "td,dkh->kth", text_emb, text_kv, preferred_element_type=jnp.float32
    ).astype(jnp.bfloat16)
    rows = give_back(attend(heads, text, text_len))
    columns = gradient(rows, output_cotangent[0])
    output_weight_gradient = lax.psum_scatter(
        columns, "seq", scatter_dimension=0, tiled=True
    ).astype(jnp.float32)
    projected = jnp.dot(rows, weight, preferred_element_type=jnp.float32)
    return (projected.astype(jnp.bfloat16)[None], output_weight_gradient)


def solution(mesh):
    placed = (
        P("dp", None, "seq"),
        P("seq", None),
        P(),
        P("dp"),
        P(None, None, "seq"),
        P("dp", "seq", None, None),
        P("seq", None),
        P("dp", "seq", None),
    )
    return jax.shard_map(
        shards,
        mesh=mesh,
        in_specs=placed,
        out_specs=(P("dp", "seq", None), P("seq", "dp")),
        check_vma=False,
    )
```

```python
import functools
import math

import jax
import jax.numpy as jnp
from jax import lax
from jax.experimental import pallas as pl
from jax.experimental.pallas import tpu as pltpu
from jax.sharding import PartitionSpec as P

HD = 128
MESH = pl.DeviceIdType.MESH
ANY = pl.BlockSpec(memory_space=pl.ANY)


def collect_kernel(n, chips, qkv, rows, heads, weight, z_s, z_r, q_s, q_r, p_s, p_r, c_s, c_r, own):
    me, dp = lax.axis_index("seq"), lax.axis_index("dp")
    chip, core = dp // 2, dp % 2
    other = 2 * chip + 1 - core
    tokens = qkv.shape[1]
    width = heads.shape[2]
    block = rows.shape[0]
    share = block // (2 * chips)

    barrier = pltpu.get_barrier_semaphore()
    for k in range(1, n):
        to = lax.rem(me + k, n)
        pl.semaphore_signal(barrier, inc=1, device_id=(dp, to), device_id_type=MESH)
    for k in range(1, chips):
        to = 2 * lax.rem(chip + k, chips) + core
        pl.semaphore_signal(barrier, inc=1, device_id=(to, me), device_id_type=MESH)
    pl.semaphore_signal(barrier, inc=1, device_id=(other, me), device_id_type=MESH)
    pl.semaphore_wait(barrier, n - 1 + chips - 1 + 1)

    def remote(src, dst, send, recv, to):
        return pltpu.make_async_remote_copy(
            src_ref=src, dst_ref=dst, send_sem=send, recv_sem=recv, device_id=to, device_id_type=MESH
        )

    def piece(s, d):
        start = pl.multiple_of(s * block + d * share, share)
        return weight.at[pl.ds(start, share)]

    def columns(s):
        return pl.ds(pl.multiple_of(s * width, width), width)

    mine = pl.ds(pl.multiple_of(me * tokens, tokens), tokens)
    fetch, tokens_out = [], []
    for k in range(1, n):
        to = lax.rem(me + k, n)
        fetch.append(
            remote(
                rows.at[pl.ds(pl.multiple_of(dp * share, share), share)],
                piece(me, dp), z_s.at[k - 1], z_r.at[k - 1], (dp, to),
            )
        )
        fetch[-1].start()
    for k in range(1, n):
        to = lax.rem(me + k, n)
        tokens_out.append(
            remote(
                qkv.at[:, :, columns(to)], heads.at[:, mine], q_s.at[k - 1], q_r.at[k - 1], (dp, to)
            )
        )
        tokens_out[-1].start()
    stay = [
        pltpu.make_async_copy(qkv.at[:, :, columns(me)], heads.at[:, mine], own.at[0]),
        pltpu.make_async_copy(
            rows, weight.at[pl.ds(pl.multiple_of(me * block, block), block)], own.at[1]
        ),
    ]
    for copy in stay:
        copy.start()

    plane, cores = [], []
    for k in range(1, n):
        fetch[k - 1].wait_recv()
        source = lax.rem(me - k + n, n)
        held = piece(source, dp)
        for c in range(1, chips):
            to = 2 * lax.rem(chip + c, chips) + core
            plane.append(remote(held, held, p_s.at[k - 1, c - 1], p_r.at[k - 1, c - 1], (to, me)))
            plane[-1].start()
        cores.append(remote(held, held, c_s.at[k - 1, 0], c_r.at[k - 1, 0], (other, me)))
        cores[-1].start()
    for k in range(1, n):
        source = lax.rem(me - k + n, n)
        for c in range(1, chips):
            plane[(k - 1) * (chips - 1) + c - 1].wait_recv()
            held = piece(source, 2 * lax.rem(chip - c + chips, chips) + core)
            cores.append(remote(held, held, c_s.at[k - 1, c], c_r.at[k - 1, c], (other, me)))
            cores[-1].start()
    for copy in fetch + plane:
        copy.wait_send()
    for copy in cores + tokens_out + stay:
        copy.wait()


def collect(lat_qkv, output_weight):
    n, chips = lax.axis_size("seq"), lax.axis_size("dp") // 2
    _, tokens, _, wide = lat_qkv.shape
    block, features = output_weight.shape
    dma = pltpu.SemaphoreType.DMA
    return pl.pallas_call(
        functools.partial(collect_kernel, n, chips),
        out_shape=(
            jax.ShapeDtypeStruct((3, n * tokens, wide // n), lat_qkv.dtype),
            jax.ShapeDtypeStruct((n * block, features), output_weight.dtype),
        ),
        in_specs=[ANY, ANY],
        out_specs=(ANY, ANY),
        scratch_shapes=[
            dma((n - 1,)), dma((n - 1,)), dma((n - 1,)), dma((n - 1,)),
            dma((n - 1, chips - 1)), dma((n - 1, chips - 1)),
            dma((n - 1, chips)), dma((n - 1, chips)), dma((2,)),
        ],
        compiler_params=pltpu.CompilerParams(collective_id=0, has_side_effects=True),
        cost_estimate=pl.CostEstimate(flops=0, bytes_accessed=300_000_000, transcendentals=0),
    )(jnp.transpose(lat_qkv[0], (1, 0, 2)), output_weight)


def return_kernel(n, attn, rows, send, recv, own):
    me, dp = lax.axis_index("seq"), lax.axis_index("dp")
    tokens, width = rows.shape[0], attn.shape[1]
    barrier = pltpu.get_barrier_semaphore()
    for k in range(1, n):
        to = lax.rem(me + k, n)
        pl.semaphore_signal(barrier, inc=1, device_id=(dp, to), device_id_type=MESH)
    pl.semaphore_wait(barrier, n - 1)
    mine = rows.at[:, pl.ds(pl.multiple_of(me * width, width), width)]

    def part(s):
        return attn.at[pl.ds(pl.multiple_of(s * tokens, tokens), tokens)]

    copies = []
    for k in range(1, n):
        to = lax.rem(me + k, n)
        copies.append(
            pltpu.make_async_remote_copy(
                src_ref=part(to), dst_ref=mine, send_sem=send.at[k - 1], recv_sem=recv.at[k - 1],
                device_id=(dp, to), device_id_type=MESH,
            )
        )
    copies.append(pltpu.make_async_copy(part(me), mine, own))
    for copy in copies:
        copy.start()
    for copy in copies:
        copy.wait()


def give_back(attn):
    n = lax.axis_size("seq")
    latent, width = attn.shape
    dma = pltpu.SemaphoreType.DMA
    return pl.pallas_call(
        functools.partial(return_kernel, n),
        out_shape=jax.ShapeDtypeStruct((latent // n, width * n), attn.dtype),
        in_specs=[ANY],
        out_specs=ANY,
        scratch_shapes=[dma((n - 1,)), dma((n - 1,)), dma],
        compiler_params=pltpu.CompilerParams(collective_id=1, has_side_effects=True),
        cost_estimate=pl.CostEstimate(flops=0, bytes_accessed=60_000_000, transcendentals=0),
    )(attn)


def attend_kernel(length, q, k, v, text_k, text_v, out):
    turned = (((1,), (1,)), ((), ()))
    query = q[0]
    latent = lax.dot_general(query, k[0], turned, preferred_element_type=jnp.float32)
    text = lax.dot_general(query, text_k[0], turned, preferred_element_type=jnp.float32)
    place = lax.broadcasted_iota(jnp.int32, text.shape, 1)
    text = jnp.where(place < length[0], text, -1e30)
    top = jnp.maximum(jnp.max(latent, -1, keepdims=True), jnp.max(text, -1, keepdims=True))
    scale = HD ** (-0.5) * math.log2(math.e)
    latent = jnp.exp2((latent - top) * scale)
    text = jnp.exp2((text - top) * scale)
    total = jnp.sum(latent, -1, keepdims=True) + jnp.sum(text, -1, keepdims=True)
    result = jnp.dot(latent.astype(jnp.bfloat16), v[0], preferred_element_type=jnp.float32)
    result += jnp.dot(text.astype(jnp.bfloat16), text_v[0], preferred_element_type=jnp.float32)
    out[...] = (result / total).astype(out.dtype)


def attend(heads, text, text_len):
    _, latent, width = heads.shape
    count = text.shape[1]
    rows = min(512, latent)

    def block(index, size):
        return pl.BlockSpec((1, size, HD), lambda h, i: (index, 0, h))

    return pl.pallas_call(
        attend_kernel,
        grid=(width // HD, latent // rows),
        in_specs=[
            pl.BlockSpec(memory_space=pltpu.SMEM),
            pl.BlockSpec((1, rows, HD), lambda h, i: (0, i, h)),
            block(1, latent), block(2, latent), block(0, count), block(1, count),
        ],
        out_specs=pl.BlockSpec((rows, HD), lambda h, i: (i, h)),
        out_shape=jax.ShapeDtypeStruct((latent, width), jnp.bfloat16),
        compiler_params=pltpu.CompilerParams(vmem_limit_bytes=40 * 2**20),
    )(text_len, heads, heads, heads, text, text)


def gradient_kernel(
    n, chips, attn, cotangent, out, turned, give, got, keep, land, part, come,
    g_s, g_r, k_s, k_r, s_s, s_r
):
    me, dp = lax.axis_index("seq"), lax.axis_index("dp")
    chip, core = dp // 2, dp % 2
    other = 2 * chip + 1 - core
    wide, block = attn.shape[1], out.shape[0]
    tile = math.gcd(block, 512)

    barrier = pltpu.get_barrier_semaphore()
    for k in range(1, chips):
        to = 2 * lax.rem(chip + k, chips) + core
        pl.semaphore_signal(barrier, inc=1, device_id=(to, me), device_id_type=MESH)
    pl.semaphore_signal(barrier, inc=1, device_id=(other, me), device_id_type=MESH)
    for r in range(1, n):
        to = lax.rem(me + r, n)
        pl.semaphore_signal(barrier, inc=1, device_id=(dp, to), device_id_type=MESH)
    turned[...] = attn[...].T
    pl.semaphore_wait(barrier, chips + n - 1)

    def remote(src, dst, send, recv, to):
        return pltpu.make_async_remote_copy(
            src_ref=src, dst_ref=dst, send_sem=send, recv_sem=recv, device_id=to, device_id_type=MESH
        )

    def tiles(body, first, count):
        def step(t, carry):
            body(pl.ds(pl.multiple_of(first + t * tile, tile), tile))
            return carry

        lax.fori_loop(0, count // tile, step, 0)

    def term(rows, index):
        return jnp.dot(turned[rows, :], cotangent[index], preferred_element_type=jnp.float32)

    order = list(range(1, chips)) + [0]
    gives, keeps = {}, []
    for k in order:
        index = 2 * lax.rem(chip + k, chips) + 1 - core

        def fill(rows):
            give[k, rows, :] = term(rows, index).astype(give.dtype)

        tiles(fill, 0, wide)
        gives[k] = remote(give.at[k], got.at[k], g_s.at[k], g_r.at[k], (other, me))
        gives[k].start()
    turns = list(range(1, n)) + [0]
    for r in turns:
        first = pl.multiple_of(lax.rem(me + r, n) * block, block)
        rows_of = pl.ds(first, block)
        for k in range(1, chips):
            index = 2 * lax.rem(chip + k, chips) + core
            if r == turns[0]:
                gives[k].wait_recv()

            def add(rows):
                both = term(rows, index) + got[k, rows, :].astype(jnp.float32)
                keep[k - 1, rows, :] = both.astype(keep.dtype)

            tiles(add, first, block)
            keeps.append(
                remote(
                    keep.at[k - 1, rows_of], land.at[k - 1, rows_of],
                    k_s.at[k - 1, r], k_r.at[k - 1, r], (index, me),
                )
            )
            keeps[-1].start()
    gives[0].wait_recv()

    def total(rows):
        value = term(rows, dp) + got[0, rows, :].astype(jnp.float32)
        for k in range(1, chips):
            value += land[k - 1, rows, :].astype(jnp.float32)
        return value

    sends = []
    for turn, r in enumerate(turns):
        to = lax.rem(me + r, n)
        rows = pl.ds(pl.multiple_of(to * block, block), block)
        for k in range(1, chips):
            keeps[turn * (chips - 1) + k - 1].wait_recv()
        if r:
            part[r - 1] = total(rows).astype(part.dtype)
            sends.append(remote(part.at[r - 1], come.at[r - 1], s_s.at[r - 1], s_r.at[r - 1], (dp, to)))
            sends[-1].start()
        else:
            value = total(rows)
            for copy in sends:
                copy.wait_recv()
            for k in range(1, n):
                value += come[k - 1].astype(jnp.float32)
            out[...] = value
    for copy in list(gives.values()) + keeps + sends:
        copy.wait_send()


def gradient(attn, cotangent):
    n, parts = lax.axis_size("seq"), lax.axis_size("dp")
    chips = parts // 2
    tokens, wide = attn.shape
    width = cotangent.shape[1] // parts
    cotangent = jnp.transpose(cotangent.reshape(tokens, parts, width), (1, 0, 2))
    vmem = pl.BlockSpec(memory_space=pltpu.VMEM)
    dma = pltpu.SemaphoreType.DMA
    return pl.pallas_call(
        functools.partial(gradient_kernel, n, chips),
        in_specs=[vmem, vmem],
        out_specs=vmem,
        out_shape=jax.ShapeDtypeStruct((wide // n, width), jnp.float32),
        scratch_shapes=[
            pltpu.VMEM((wide, tokens), jnp.bfloat16),
            pltpu.VMEM((chips, wide, width), jnp.bfloat16),
            pltpu.VMEM((chips, wide, width), jnp.bfloat16),
            pltpu.VMEM((chips - 1, wide, width), jnp.bfloat16),
            pltpu.VMEM((chips - 1, wide, width), jnp.bfloat16),
            pltpu.VMEM((n - 1, wide // n, width), jnp.bfloat16),
            pltpu.VMEM((n - 1, wide // n, width), jnp.bfloat16),
            dma((chips,)), dma((chips,)), dma((chips - 1, n)), dma((chips - 1, n)),
            dma((n - 1,)), dma((n - 1,)),
        ],
        compiler_params=pltpu.CompilerParams(
            collective_id=2, has_side_effects=True, vmem_limit_bytes=52 * 2**20
        ),
        cost_estimate=pl.CostEstimate(flops=0, bytes_accessed=200_000_000, transcendentals=0),
    )(attn, cotangent)


def shards(
    enc_hidden, enc_wo, enc_gain, text_len, text_kv, lat_qkv, output_weight, output_cotangent
):
    partial_value = jnp.dot(
        enc_hidden[0], enc_wo, preferred_element_type=jnp.float32
    ).astype(jnp.bfloat16)
    partial_value, lat_qkv = lax.optimization_barrier((partial_value, lat_qkv))
    summed = lax.psum(partial_value, "seq")
    heads, weight = collect(lat_qkv, output_weight)
    heads, output_cotangent = lax.optimization_barrier((heads, output_cotangent))
    summed = summed.astype(jnp.float32)
    meansq = jnp.mean(summed * summed, -1, keepdims=True)
    text_emb = (summed * lax.rsqrt(meansq + 1e-06) * enc_gain).astype(jnp.bfloat16)
    text = jnp.einsum(
        "td,dkh->kth", text_emb, text_kv, preferred_element_type=jnp.float32
    ).astype(jnp.bfloat16)
    rows = give_back(attend(heads, text, text_len))
    output_weight_gradient = gradient(rows, output_cotangent[0])
    projected = jnp.dot(rows, weight, preferred_element_type=jnp.float32)
    return (projected.astype(jnp.bfloat16)[None], output_weight_gradient)


def solution(mesh):
    placed = (
        P("dp", None, "seq"),
        P("seq", None),
        P(),
        P("dp"),
        P(None, None, "seq"),
        P("dp", "seq", None, None),
        P("seq", None),
        P("dp", "seq", None),
    )
    return jax.shard_map(
        shards,
        mesh=mesh,
        in_specs=placed,
        out_specs=(P("dp", "seq", None), P("seq", "dp")),
        check_vma=False,
    )
```

```python
import functools
import math

import jax
import jax.numpy as jnp
from jax import lax
from jax.experimental import pallas as pl
from jax.experimental.pallas import tpu as pltpu
from jax.sharding import PartitionSpec as P

HD = 128
MESH = pl.DeviceIdType.MESH
ANY = pl.BlockSpec(memory_space=pl.ANY)


def collect_kernel(n, chips, qkv, rows, heads, weight, z_s, z_r, q_s, q_r, p_s, p_r, c_s, c_r, own):
    me, dp = lax.axis_index("seq"), lax.axis_index("dp")
    chip, core = dp // 2, dp % 2
    other = 2 * chip + 1 - core
    tokens = qkv.shape[1]
    width = heads.shape[2]
    block = rows.shape[0]
    share = block // (2 * chips)

    barrier = pltpu.get_barrier_semaphore()
    for k in range(1, n):
        to = lax.rem(me + k, n)
        pl.semaphore_signal(barrier, inc=1, device_id=(dp, to), device_id_type=MESH)
    for k in range(1, chips):
        to = 2 * lax.rem(chip + k, chips) + core
        pl.semaphore_signal(barrier, inc=1, device_id=(to, me), device_id_type=MESH)
    pl.semaphore_signal(barrier, inc=1, device_id=(other, me), device_id_type=MESH)
    pl.semaphore_wait(barrier, n - 1 + chips - 1 + 1)

    def remote(src, dst, send, recv, to):
        return pltpu.make_async_remote_copy(
            src_ref=src, dst_ref=dst, send_sem=send, recv_sem=recv, device_id=to, device_id_type=MESH
        )

    def piece(s, d):
        start = pl.multiple_of(s * block + d * share, share)
        return weight.at[pl.ds(start, share)]

    def columns(s):
        return pl.ds(pl.multiple_of(s * width, width), width)

    mine = pl.ds(pl.multiple_of(me * tokens, tokens), tokens)
    fetch, tokens_out = [], []
    for k in range(1, n):
        to = lax.rem(me + k, n)
        fetch.append(
            remote(
                rows.at[pl.ds(pl.multiple_of(dp * share, share), share)],
                piece(me, dp), z_s.at[k - 1], z_r.at[k - 1], (dp, to),
            )
        )
        fetch[-1].start()
    for k in range(1, n):
        to = lax.rem(me + k, n)
        tokens_out.append(
            remote(
                qkv.at[:, :, columns(to)], heads.at[:, mine], q_s.at[k - 1], q_r.at[k - 1], (dp, to)
            )
        )
        tokens_out[-1].start()
    stay = [
        pltpu.make_async_copy(qkv.at[:, :, columns(me)], heads.at[:, mine], own.at[0]),
        pltpu.make_async_copy(
            rows, weight.at[pl.ds(pl.multiple_of(me * block, block), block)], own.at[1]
        ),
    ]
    for copy in stay:
        copy.start()

    plane, cores = [], []
    for k in range(1, n):
        fetch[k - 1].wait_recv()
        source = lax.rem(me - k + n, n)
        held = piece(source, dp)
        for c in range(1, chips):
            to = 2 * lax.rem(chip + c, chips) + core
            plane.append(remote(held, held, p_s.at[k - 1, c - 1], p_r.at[k - 1, c - 1], (to, me)))
            plane[-1].start()
        cores.append(remote(held, held, c_s.at[k - 1, 0], c_r.at[k - 1, 0], (other, me)))
        cores[-1].start()
    for k in range(1, n):
        source = lax.rem(me - k + n, n)
        for c in range(1, chips):
            plane[(k - 1) * (chips - 1) + c - 1].wait_recv()
            held = piece(source, 2 * lax.rem(chip - c + chips, chips) + core)
            cores.append(remote(held, held, c_s.at[k - 1, c], c_r.at[k - 1, c], (other, me)))
            cores[-1].start()
    for copy in fetch + plane:
        copy.wait_send()
    for copy in cores + tokens_out + stay:
        copy.wait()


def collect(lat_qkv, output_weight):
    n, chips = lax.axis_size("seq"), lax.axis_size("dp") // 2
    _, tokens, _, wide = lat_qkv.shape
    block, features = output_weight.shape
    dma = pltpu.SemaphoreType.DMA
    return pl.pallas_call(
        functools.partial(collect_kernel, n, chips),
        out_shape=(
            jax.ShapeDtypeStruct((3, n * tokens, wide // n), lat_qkv.dtype),
            jax.ShapeDtypeStruct((n * block, features), output_weight.dtype),
        ),
        in_specs=[ANY, ANY],
        out_specs=(ANY, ANY),
        scratch_shapes=[
            dma((n - 1,)), dma((n - 1,)), dma((n - 1,)), dma((n - 1,)),
            dma((n - 1, chips - 1)), dma((n - 1, chips - 1)),
            dma((n - 1, chips)), dma((n - 1, chips)), dma((2,)),
        ],
        compiler_params=pltpu.CompilerParams(collective_id=0, has_side_effects=True),
        cost_estimate=pl.CostEstimate(flops=0, bytes_accessed=300_000_000, transcendentals=0),
    )(jnp.transpose(lat_qkv[0], (1, 0, 2)), output_weight)


def return_kernel(n, attn, rows, send, recv, own):
    me, dp = lax.axis_index("seq"), lax.axis_index("dp")
    tokens, width = rows.shape[0], attn.shape[1]
    barrier = pltpu.get_barrier_semaphore()
    for k in range(1, n):
        to = lax.rem(me + k, n)
        pl.semaphore_signal(barrier, inc=1, device_id=(dp, to), device_id_type=MESH)
    pl.semaphore_wait(barrier, n - 1)
    mine = rows.at[:, pl.ds(pl.multiple_of(me * width, width), width)]

    def part(s):
        return attn.at[pl.ds(pl.multiple_of(s * tokens, tokens), tokens)]

    copies = []
    for k in range(1, n):
        to = lax.rem(me + k, n)
        copies.append(
            pltpu.make_async_remote_copy(
                src_ref=part(to), dst_ref=mine, send_sem=send.at[k - 1], recv_sem=recv.at[k - 1],
                device_id=(dp, to), device_id_type=MESH,
            )
        )
    copies.append(pltpu.make_async_copy(part(me), mine, own))
    for copy in copies:
        copy.start()
    for copy in copies:
        copy.wait()


def give_back(attn):
    n = lax.axis_size("seq")
    latent, width = attn.shape
    dma = pltpu.SemaphoreType.DMA
    return pl.pallas_call(
        functools.partial(return_kernel, n),
        out_shape=jax.ShapeDtypeStruct((latent // n, width * n), attn.dtype),
        in_specs=[ANY],
        out_specs=ANY,
        scratch_shapes=[dma((n - 1,)), dma((n - 1,)), dma],
        compiler_params=pltpu.CompilerParams(collective_id=1, has_side_effects=True),
        cost_estimate=pl.CostEstimate(flops=0, bytes_accessed=60_000_000, transcendentals=0),
    )(attn)


def attend_kernel(length, q, k, v, text_k, text_v, out):
    turned = (((1,), (1,)), ((), ()))
    query = q[0]
    latent = lax.dot_general(query, k[0], turned, preferred_element_type=jnp.float32)
    text = lax.dot_general(query, text_k[0], turned, preferred_element_type=jnp.float32)
    place = lax.broadcasted_iota(jnp.int32, text.shape, 1)
    text = jnp.where(place < length[0], text, -1e30)
    top = jnp.maximum(jnp.max(latent, -1, keepdims=True), jnp.max(text, -1, keepdims=True))
    scale = HD ** (-0.5) * math.log2(math.e)
    latent = jnp.exp2((latent - top) * scale)
    text = jnp.exp2((text - top) * scale)
    total = jnp.sum(latent, -1, keepdims=True) + jnp.sum(text, -1, keepdims=True)
    result = jnp.dot(latent.astype(jnp.bfloat16), v[0], preferred_element_type=jnp.float32)
    result += jnp.dot(text.astype(jnp.bfloat16), text_v[0], preferred_element_type=jnp.float32)
    out[...] = (result / total).astype(out.dtype)


def attend(heads, text, text_len):
    _, latent, width = heads.shape
    count = text.shape[1]
    rows = min(512, latent)

    def block(index, size):
        return pl.BlockSpec((1, size, HD), lambda h, i: (index, 0, h))

    return pl.pallas_call(
        attend_kernel,
        grid=(width // HD, latent // rows),
        in_specs=[
            pl.BlockSpec(memory_space=pltpu.SMEM),
            pl.BlockSpec((1, rows, HD), lambda h, i: (0, i, h)),
            block(1, latent), block(2, latent), block(0, count), block(1, count),
        ],
        out_specs=pl.BlockSpec((rows, HD), lambda h, i: (i, h)),
        out_shape=jax.ShapeDtypeStruct((latent, width), jnp.bfloat16),
        compiler_params=pltpu.CompilerParams(vmem_limit_bytes=40 * 2**20),
    )(text_len, heads, heads, heads, text, text)


def gradient_kernel(
    n, chips, attn, cotangent, weight, out, projected, turned, give, got, keep, land, part, come,
    held, w_s,
    g_s, g_r, k_s, k_r, s_s, s_r
):
    me, dp = lax.axis_index("seq"), lax.axis_index("dp")
    chip, core = dp // 2, dp % 2
    other = 2 * chip + 1 - core
    wide, block = attn.shape[1], out.shape[0]
    tile = math.gcd(block, 512)

    barrier = pltpu.get_barrier_semaphore()
    for k in range(1, chips):
        to = 2 * lax.rem(chip + k, chips) + core
        pl.semaphore_signal(barrier, inc=1, device_id=(to, me), device_id_type=MESH)
    pl.semaphore_signal(barrier, inc=1, device_id=(other, me), device_id_type=MESH)
    for r in range(1, n):
        to = lax.rem(me + r, n)
        pl.semaphore_signal(barrier, inc=1, device_id=(dp, to), device_id_type=MESH)
    bring = pltpu.make_async_copy(weight, held, w_s)
    bring.start()
    turned[...] = attn[...].T
    pl.semaphore_wait(barrier, chips + n - 1)

    def remote(src, dst, send, recv, to):
        return pltpu.make_async_remote_copy(
            src_ref=src, dst_ref=dst, send_sem=send, recv_sem=recv, device_id=to, device_id_type=MESH
        )

    def tiles(body, first, count):
        def step(t, carry):
            body(pl.ds(pl.multiple_of(first + t * tile, tile), tile))
            return carry

        lax.fori_loop(0, count // tile, step, 0)

    def term(rows, index):
        return jnp.dot(turned[rows, :], cotangent[index], preferred_element_type=jnp.float32)

    order = list(range(1, chips)) + [0]
    gives, keeps = {}, []
    for k in order:
        index = 2 * lax.rem(chip + k, chips) + 1 - core

        def fill(rows):
            give[k, rows, :] = term(rows, index).astype(give.dtype)

        tiles(fill, 0, wide)
        gives[k] = remote(give.at[k], got.at[k], g_s.at[k], g_r.at[k], (other, me))
        gives[k].start()
    turns = list(range(1, n)) + [0]
    for r in turns:
        first = pl.multiple_of(lax.rem(me + r, n) * block, block)
        rows_of = pl.ds(first, block)
        for k in range(1, chips):
            index = 2 * lax.rem(chip + k, chips) + core
            if r == turns[0]:
                gives[k].wait_recv()

            def add(rows):
                both = term(rows, index) + got[k, rows, :].astype(jnp.float32)
                keep[k - 1, rows, :] = both.astype(keep.dtype)

            tiles(add, first, block)
            keeps.append(
                remote(
                    keep.at[k - 1, rows_of], land.at[k - 1, rows_of],
                    k_s.at[k - 1, r], k_r.at[k - 1, r], (index, me),
                )
            )
            keeps[-1].start()
    bring.wait()
    step_width = math.gcd(projected.shape[1], 512)

    def project(t, carry):
        cols = pl.ds(pl.multiple_of(t * step_width, step_width), step_width)
        projected[:, cols] = jnp.dot(
            attn[...], held[:, cols], preferred_element_type=jnp.float32
        ).astype(projected.dtype)
        return carry

    lax.fori_loop(0, projected.shape[1] // step_width, project, 0)
    gives[0].wait_recv()

    def total(rows):
        value = term(rows, dp) + got[0, rows, :].astype(jnp.float32)
        for k in range(1, chips):
            value += land[k - 1, rows, :].astype(jnp.float32)
        return value

    sends = []
    for turn, r in enumerate(turns):
        to = lax.rem(me + r, n)
        rows = pl.ds(pl.multiple_of(to * block, block), block)
        for k in range(1, chips):
            keeps[turn * (chips - 1) + k - 1].wait_recv()
        if r:
            part[r - 1] = total(rows).astype(part.dtype)
            sends.append(remote(part.at[r - 1], come.at[r - 1], s_s.at[r - 1], s_r.at[r - 1], (dp, to)))
            sends[-1].start()
        else:
            value = total(rows)
            for copy in sends:
                copy.wait_recv()
            for k in range(1, n):
                value += come[k - 1].astype(jnp.float32)
            out[...] = value
    for copy in list(gives.values()) + keeps + sends:
        copy.wait_send()


def gradient(attn, cotangent, weight):
    n, parts = lax.axis_size("seq"), lax.axis_size("dp")
    chips = parts // 2
    tokens, wide = attn.shape
    width = cotangent.shape[1] // parts
    cotangent = jnp.transpose(cotangent.reshape(tokens, parts, width), (1, 0, 2))
    vmem = pl.BlockSpec(memory_space=pltpu.VMEM)
    dma = pltpu.SemaphoreType.DMA
    return pl.pallas_call(
        functools.partial(gradient_kernel, n, chips),
        in_specs=[vmem, vmem, ANY],
        out_specs=(vmem, vmem),
        out_shape=(
            jax.ShapeDtypeStruct((wide // n, width), jnp.float32),
            jax.ShapeDtypeStruct((tokens, weight.shape[1]), jnp.bfloat16),
        ),
        scratch_shapes=[
            pltpu.VMEM((wide, tokens), jnp.bfloat16),
            pltpu.VMEM((chips, wide, width), jnp.bfloat16),
            pltpu.VMEM((chips, wide, width), jnp.bfloat16),
            pltpu.VMEM((chips - 1, wide, width), jnp.bfloat16),
            pltpu.VMEM((chips - 1, wide, width), jnp.bfloat16),
            pltpu.VMEM((n - 1, wide // n, width), jnp.bfloat16),
            pltpu.VMEM((n - 1, wide // n, width), jnp.bfloat16),
            pltpu.VMEM(weight.shape, jnp.bfloat16),
            dma,
            dma((chips,)), dma((chips,)), dma((chips - 1, n)), dma((chips - 1, n)),
            dma((n - 1,)), dma((n - 1,)),
        ],
        compiler_params=pltpu.CompilerParams(
            collective_id=2, has_side_effects=True, vmem_limit_bytes=58 * 2**20
        ),
        cost_estimate=pl.CostEstimate(flops=0, bytes_accessed=200_000_000, transcendentals=0),
    )(attn, cotangent, weight)


def shards(
    enc_hidden, enc_wo, enc_gain, text_len, text_kv, lat_qkv, output_weight, output_cotangent
):
    partial_value = jnp.dot(
        enc_hidden[0], enc_wo, preferred_element_type=jnp.float32
    ).astype(jnp.bfloat16)
    partial_value, lat_qkv = lax.optimization_barrier((partial_value, lat_qkv))
    summed = lax.psum(partial_value, "seq")
    heads, weight = collect(lat_qkv, output_weight)
    heads, output_cotangent = lax.optimization_barrier((heads, output_cotangent))
    summed = summed.astype(jnp.float32)
    meansq = jnp.mean(summed * summed, -1, keepdims=True)
    text_emb = (summed * lax.rsqrt(meansq + 1e-06) * enc_gain).astype(jnp.bfloat16)
    text = jnp.einsum(
        "td,dkh->kth", text_emb, text_kv, preferred_element_type=jnp.float32
    ).astype(jnp.bfloat16)
    rows = give_back(attend(heads, text, text_len))
    output_weight_gradient, projected = gradient(rows, output_cotangent[0], weight)
    return (projected[None], output_weight_gradient)


def solution(mesh):
    placed = (
        P("dp", None, "seq"),
        P("seq", None),
        P(),
        P("dp"),
        P(None, None, "seq"),
        P("dp", "seq", None, None),
        P("seq", None),
        P("dp", "seq", None),
    )
    return jax.shard_map(
        shards,
        mesh=mesh,
        in_specs=placed,
        out_specs=(P("dp", "seq", None), P("seq", "dp")),
        check_vma=False,
    )
```
